1024 devices in a mesh: row: 64 (over y, x), col: 16 (over z, core).
Axes of the slice: x: 8, y: 8, z: 8, core: 2. Of those that a mesh axis runs over, the one named last changes fastest.
Arguments:
- density: bfloat16 [4096, 4096], P('row', 'col'), may hold values from -1 to 1, as said below
- branches: int32 [4], replicated, may hold values from 0 to 1, as said below
- keep: int32 [4, 32, 32], replicated, may hold values from 0 to 1, as said below
Outputs:
- purified: bfloat16 [4096, 4096], P('row', 'col')
- traces: float32 [4, 2], replicated
- occupations: float32 [4096], P('row')
The draws below stay inside these ranges and needn't reach their ends.
Inputs may be any that keep to these rules, and one draw needn't show every extreme that they name: density is exactly symmetric. `branches`: exactly half of the 4 steps take the square. Each keep[s] is symmetric in its two block indices and holds 1 on every diagonal block.
All inputs are finite; a program needn't handle non-finite values.
Results may differ from the reference program's by a relative error of at most 0.0077.
Values may be sent and summed in bfloat16 or wider, within the bound.
A program may use at most 32 MiB of HBM per device.

```python
import math
import jax
import jax.numpy as jnp

B = 128
NB = 32
STEPS = 4


def draw_density(key, part):
    order = NB * B
    width = B // 2
    group_count = order // width
    first_key, second_key, third_key = jax.random.split(key, 3)
    level = jax.random.uniform(second_key, (group_count,), jnp.float32, 0.0, 1.0)
    noise = jnp.clip(jax.random.normal(first_key, (order, order), jnp.float32), -6.0, 6.0)
    values = 0.5 + 0.38 * jnp.tanh(8.0 * (level - 0.5)) / math.tanh(4.0)
    jitter = 0.03 * jax.random.uniform(third_key, (order,), jnp.float32, -1.0, 1.0)
    diagonal = jnp.repeat(values, width) + jitter
    factor = 0.18 / math.sqrt(2.0 * order)
    mirrored = (noise + noise.T) * factor
    rows_index = jnp.arange(order)[:, None]
    cols_index = jnp.arange(order)[None, :]
    full = jnp.where(rows_index == cols_index, diagonal[:, None] + 0.0 * mirrored, mirrored)
    return full.astype(jnp.bfloat16)


def draw_branches(key, part):
    order_key = jax.random.fold_in(key, 17)
    shuffled = jax.random.permutation(order_key, jnp.arange(STEPS, dtype=jnp.int32))
    return (shuffled < STEPS // 2).astype(jnp.int32)


def draw_keep(key, part):
    draws = jax.random.randint(key, (STEPS, NB, NB), 0, 8)
    upper = (draws < 7).astype(jnp.int32)
    rows_index = jnp.arange(NB)[:, None]
    cols_index = jnp.arange(NB)[None, :]
    lower = jnp.swapaxes(upper, 1, 2)
    joined = jnp.where(rows_index < cols_index, upper, lower)
    return jnp.where(rows_index == cols_index, jnp.ones_like(joined), joined).astype(jnp.int32)


def setup_inputs(seed: int = 0) -> dict:
    arg_keys = jax.random.split(jax.random.key(seed), 4)
    return {
        "density": draw_density(jax.random.fold_in(arg_keys[3], 71), 0),
        "branches": draw_branches(jax.random.fold_in(arg_keys[3], 71), 0),
        "keep": draw_keep(jax.random.fold_in(arg_keys[3], 71), 0),
    }


def reference(density, branches, keep):
    order = NB * B
    current = density
    collected = []
    kept = jnp.zeros((order, order), jnp.float32)
    for section in range(STEPS):
        square = jnp.dot(current, current, preferred_element_type=jnp.float32)
        trace_one = jnp.sum(jnp.diagonal(current.astype(jnp.float32)))
        trace_two = jnp.sum(jnp.diagonal(square))
        grown = jnp.where(branches[section] == 1, square, 2.0 * current.astype(jnp.float32) - square)
        block_keep = jnp.repeat(jnp.repeat(keep[section], B, axis=0), B, axis=1).astype(jnp.float32)
        kept = grown * block_keep
        current = kept.astype(jnp.bfloat16)
        collected.append(jnp.stack([trace_one, trace_two]) / order)
    occupations = jnp.diagonal(kept)
    positions = jnp.arange(order)
    purified = current.at[positions, positions].set(jnp.zeros((order,), jnp.bfloat16))
    return purified, jnp.stack(collected), occupations
```

```python
import functools

import jax
import jax.numpy as jnp
from jax import lax
from jax.experimental import pallas as pl
from jax.experimental.pallas import tpu as pltpu
from jax.sharding import PartitionSpec as P

B = 128
LANES = 128
STEPS = 4
H = 2
MESH = pl.DeviceIdType.MESH
F32 = jnp.float32
BF16 = jnp.bfloat16
NT = (((1,), (1,)), ((), ()))


def kernel(G, bs, dens, branches_in, keep_in, out, traces, occ,
           a2, a3, p1, n1, h1, d1, cur, es, rr, vz, vs, vy, branches, keep,
           in_s, ax_s, ax_r, au_s, au_r, rs_s, rs_r, dd_s, dd_r, es_s, es_r, vs_s, vs_r, sb_s, sb_r):
    half, slab = bs // 2, bs // G
    order = G * bs
    row, col = lax.axis_index("row"), lax.axis_index("col")
    x, y, z, c = lax.rem(row, G), row // G, col // 2, lax.rem(col, 2)
    xs = pl.multiple_of(x * slab, slab)
    mine = pl.multiple_of(c * half, half)
    theirs = pl.multiple_of((1 - c) * half, half)

    def dev(ax, ay, az, ac):
        return {"row": ay * G + ax, "col": az * 2 + ac}

    far_first = sorted(range(1, G), key=lambda d: -min(d, G - d))
    pos = {"x": {d: lax.rem(x + d, G) for d in far_first},
           "y": {d: lax.rem(y + d, G) for d in far_first},
           "z": {d: lax.rem(z + d, G) for d in far_first}}
    ids = {"x": {d: dev(pos["x"][d], y, z, c) for d in far_first},
           "y": {d: dev(x, pos["y"][d], z, c) for d in far_first},
           "z": {d: dev(x, y, pos["z"][d], c) for d in far_first}}
    here = {"x": x, "y": y, "z": z}
    sib = dev(x, y, z, 1 - c)

    def copy(src, dst, ssem, rsem, target):
        return pltpu.make_async_remote_copy(
            src_ref=src, dst_ref=dst, send_sem=ssem, recv_sem=rsem,
            device_id=target, device_id_type=MESH)

    def got(ref, sem):
        copy(ref, ref, sem, sem, sib).wait_recv()

    def left(ref, sem):
        copy(ref, ref, sem, sem, sib).wait_send()

    fetch = [pltpu.make_async_copy(dens, a2.at[0, pl.ds(xs, slab)], in_s.at[0]),
             pltpu.make_async_copy(dens, a3.at[0, pl.ds(pl.multiple_of(y * slab, slab), slab)], in_s.at[1]),
             pltpu.make_async_copy(keep_in, keep, in_s.at[2]),
             pltpu.make_async_copy(branches_in, branches, in_s.at[3])]
    for cp in fetch:
        cp.start()
    barrier = pltpu.get_barrier_semaphore()
    for d in far_first:
        for axis in ("x", "y", "z"):
            pl.semaphore_signal(barrier, inc=1, device_id=ids[axis][d], device_id_type=MESH)
    pl.semaphore_signal(barrier, inc=1, device_id=sib, device_id_type=MESH)
    fetch[0].wait()
    fetch[1].wait()
    pl.semaphore_wait(barrier, 3 * (G - 1) + 1)

    sub = slab // H
    line = a2.at[0, pl.ds(0, (G - 1) * slab)]

    def gather(p, axis, h):
        two = a2.at[p, pl.ds(pl.multiple_of(xs + h * sub, sub), sub)]
        three = a3.at[p, pl.ds(pl.multiple_of(here[axis] * slab + h * sub, sub), sub)]
        for d in far_first:
            copy(two, two, ax_s, ax_r.at[p], ids["x"][d]).start()
            copy(three, three, au_s, au_r.at[p], ids[axis][d]).start()

    iota = functools.partial(lax.broadcasted_iota, jnp.int32)
    pick = jnp.where(iota((slab, half), 1) == x * slab - c * half + iota((slab, half), 0), 0.5, 0.0).astype(BF16)
    row_here = (x * slab) // half == c
    on_block = jnp.where(y == z, 1.0, 0.0).astype(F32)
    block_diag = jnp.where(iota((half, half), 0) == iota((half, half), 1), on_block, 0.0)

    t_one, t_two = [], []

    for h in range(H):
        gather(0, "y", h)
    fetch[2].wait()
    fetch[3].wait()

    for s in range(STEPS):
        p = s % 2
        n = 1 - p
        last = s == STEPS - 1
        au, av = ("y", "z") if p == 0 else ("z", "y")
        u, v = here[au], here[av]
        us = pl.multiple_of(u * slab, slab)
        vs_at = pl.multiple_of(v * slab, slab)

        got(line, ax_r.at[p])
        got(line, au_r.at[p])
        far = a2[p, pl.ds(theirs, half), :]
        near = a2[p, pl.ds(mine, half), :]
        h1[p] = lax.dot_general(a3[p], far, NT, preferred_element_type=F32).astype(BF16)

        @pl.when(row_here)
        def _():
            e = lax.dot_general(pick, far, NT, preferred_element_type=F32)
            own = lax.dot_general(a3[p, pl.ds(vs_at, slab), :], far, NT, preferred_element_type=F32)
            h1[p, pl.ds(vs_at, slab), :] = (own - e).astype(BF16)
            es[p] = (2.0 * e).astype(BF16)
            copy(es.at[p], cur.at[p], es_s.at[p], es_r.at[p], sib).start()

        copy(h1.at[p], d1.at[p], dd_s.at[p], dd_r.at[p], sib).start()
        n1[...] = lax.dot_general(a3[p], near, NT, preferred_element_type=F32) - (0.5 * on_block) * a3[p].astype(F32)

        @pl.when(row_here)
        def _():
            e = lax.dot_general(pick, near, NT, preferred_element_type=F32)
            n1[pl.ds(vs_at, slab), :] = n1[pl.ds(vs_at, slab), :] - e
            cur[p] = (2.0 * e).astype(BF16)

        got(d1.at[p], dd_r.at[p])
        p1[p] = (n1[...] + d1[p].astype(F32)).astype(BF16)
        if s > 0:
            left(line, rs_s)
        for h in range(H):
            for d in far_first:
                copy(p1.at[p, pl.ds(pl.multiple_of(pos[av][d] * slab + h * sub, sub), sub)],
                     rr.at[p, h, v], rs_s, rs_r.at[p, h], ids[av][d]).start()
        for h in range(H):
            rr[p, h, v] = p1[p, pl.ds(pl.multiple_of(v * slab + h * sub, sub), sub), :]

        whole = a2[p].astype(F32)
        squares = jnp.sum(whole * whole, axis=0, keepdims=True)
        diagonal = jnp.sum(a2[p, pl.ds(mine, half), :].astype(F32) * block_diag, axis=0, keepdims=True)
        t_one.append(jnp.sum(diagonal, axis=1, keepdims=True))
        t_two.append(jnp.sum(squares, axis=1, keepdims=True))

        left(line, ax_s)
        left(line, au_s)
        left(h1.at[p], dd_s.at[p])

        @pl.when(row_here)
        def _():
            left(es.at[p], es_s.at[p])

        @pl.when(jnp.logical_not(row_here))
        def _():
            got(cur.at[p], es_r.at[p])

        if last:
            lane, deep = iota((1, half), 1), iota((8, half), 0)
            trow = jnp.zeros((1, half), F32)
            for i in range(STEPS):
                trow = trow + jnp.where(lane == 2 * i, t_one[i], 0.0) + jnp.where(lane == 2 * i + 1, t_two[i], 0.0)
            vz[z] = (jnp.where(deep == 0, squares, 0.0) + jnp.where(deep == 1, diagonal, 0.0)
                     + jnp.where(deep == 2, trow, 0.0))
            for d in far_first:
                copy(vz.at[z], vz.at[z], vs_s.at[0], vs_r.at[0], ids["z"][d]).start()
            got(vz.at[pl.ds(0, G - 1)], vs_r.at[0])
            vs[c] = jnp.sum(vz[...], axis=0)
            copy(vs.at[c], vs.at[c], sb_s, sb_r, sib).start()
            got(vs.at[0], sb_r)
            vy[y] = (vs[0] + vs[1])[:, :LANES]
            for d in far_first:
                copy(vy.at[y], vy.at[y], vs_s.at[1], vs_r.at[1], ids["y"][d]).start()
            mid = jnp.where(x * slab < half, vs[0], vs[1])
            f = branches[s].astype(F32)
            grown = f * mid[0:1, :] + (1.0 - f) * (2.0 * mid[1:2, :] - mid[0:1, :])
            shown = iota((slab, half), 1) == lax.rem(x * slab, half) + iota((slab, half), 0)
            column = jnp.sum(jnp.where(shown, grown, 0.0), axis=1, keepdims=True)
            eye = iota((slab, slab), 0) == iota((slab, slab), 1)
            occ[...] = jnp.sum(jnp.where(eye, column, 0.0), axis=0, keepdims=True)

        f = branches[s].astype(F32)
        fa, fb = 2.0 * f - 1.0, 2.0 - 2.0 * f
        for h in range(H):
            rs = slice(h * sub, (h + 1) * sub)
            rb = (v * bs + x * slab + h * sub) // B
            cb = (u * bs + c * half) // B
            at2 = pl.multiple_of(xs + h * sub, sub)
            at3 = pl.multiple_of(v * slab + h * sub, sub)
            got(rr.at[p, h, pl.ds(0, G - 1)], rs_r.at[p, h])
            now = cur[p, rs, :].astype(F32)
            grown = fa * (jnp.sum(rr[p, h].astype(F32), axis=0) + now) + fb * now
            if last:
                grown = jnp.where(v * bs + x * slab + h * sub + iota((sub, half), 0)
                                  == u * bs + c * half + iota((sub, half), 1), 0.0, grown)
            for q in range(half // B):
                cs = slice(q * B, (q + 1) * B)
                new = (grown[:, cs] * keep[s, rb, cb + q].astype(F32)).astype(BF16)
                if last:
                    out[rs, cs] = new
                else:
                    a2[n, pl.ds(at2, sub), cs] = new
                    a3[n, pl.ds(at3, sub), cs] = new
            if not last:
                gather(n, av, h)

    got(vy.at[pl.ds(0, G - 1)], vs_r.at[1])
    tr = jnp.sum(vy[...], axis=0)[2:3, :] * (1.0 / order)
    lane, deep = iota((STEPS, LANES), 1), iota((STEPS, LANES), 0)
    for k in range(2):
        traces[:, k:k + 1] = jnp.sum(jnp.where(lane == 2 * deep + k, tr, 0.0), axis=1, keepdims=True)
    left(line, rs_s)
    left(vz.at[pl.ds(0, G - 1)], vs_s.at[0])
    left(vy.at[pl.ds(0, G - 1)], vs_s.at[1])
    left(vs.at[0], sb_s)


def body(G, density, branches, keep):
    slab, half = density.shape
    bs = 2 * half
    v, dma = pltpu.VMEM, pltpu.SemaphoreType.DMA
    vmem, hbm = pl.BlockSpec(memory_space=pltpu.VMEM), pl.BlockSpec(memory_space=pltpu.HBM)
    purified, traces, occ = pl.pallas_call(
        functools.partial(kernel, G, bs),
        out_shape=(jax.ShapeDtypeStruct((slab, half), BF16),
                   jax.ShapeDtypeStruct((STEPS, 2), F32),
                   jax.ShapeDtypeStruct((1, slab), F32)),
        in_specs=[hbm, hbm, hbm],
        out_specs=(vmem, vmem, vmem),
        scratch_shapes=[
            v((2, bs, half), BF16), v((2, bs, half), BF16), v((2, bs, half), BF16), v((bs, half), F32),
            v((2, bs, half), BF16), v((2, bs, half), BF16), v((2, slab, half), BF16), v((2, slab, half), BF16),
            v((2, H, G, slab // H, half), BF16),
            v((G, 8, half), F32), v((2, 8, half), F32), v((G, 8, LANES), F32),
            pltpu.SMEM(branches.shape, jnp.int32), pltpu.SMEM(keep.shape, jnp.int32),
            dma((4,)), dma, dma((2,)), dma, dma((2,)), dma, dma((2, H)), dma((2,)), dma((2,)),
            dma((2,)), dma((2,)), dma((2,)), dma((2,)), dma, dma,
        ],
        compiler_params=pltpu.CompilerParams(
            collective_id=0, has_side_effects=True, vmem_limit_bytes=60 * 1024 * 1024),
        name="purify",
    )(density, branches, keep)
    return purified, traces, occ.reshape(slab)


def solution(mesh):
    G = mesh.shape["col"] // 2
    return jax.shard_map(
        functools.partial(body, G),
        mesh=mesh,
        in_specs=(P("row", "col"), P(), P()),
        out_specs=(P("row", "col"), P(), P("row")),
        check_vma=False,
    )
```

```python
import functools

import jax
import jax.numpy as jnp
from jax import lax
from jax.experimental import pallas as pl
from jax.experimental.pallas import tpu as pltpu
from jax.sharding import PartitionSpec as P

B = 128
LANES = 128
STEPS = 4
H = 2
MESH = pl.DeviceIdType.MESH
F32 = jnp.float32
BF16 = jnp.bfloat16
NT = (((1,), (1,)), ((), ()))


def kernel(G, bs, dens, branches_in, keep_in, out, traces, occ,
           a2, a3, p1, n1, h1, d1, cur, es, ed, rr, vx, vz, vs, vy, branches, keep,
           in_s, ax_s, ax_r, au_s, au_r, rs_s, rs_r, dd_s, dd_r, es_s, es_r, vs_s, vs_r, sb_s, sb_r):
    half, slab = bs // 2, bs // G
    order = G * bs
    row, col = lax.axis_index("row"), lax.axis_index("col")
    x, y, z, c = lax.rem(row, G), row // G, col // 2, lax.rem(col, 2)
    xs = pl.multiple_of(x * slab, slab)
    mine = pl.multiple_of(c * half, half)
    theirs = pl.multiple_of((1 - c) * half, half)

    def dev(ax, ay, az, ac):
        return {"row": ay * G + ax, "col": az * 2 + ac}

    far_first = sorted(range(1, G), key=lambda d: -min(d, G - d))
    pos = {"x": {d: lax.rem(x + d, G) for d in far_first},
           "y": {d: lax.rem(y + d, G) for d in far_first},
           "z": {d: lax.rem(z + d, G) for d in far_first}}
    ids = {"x": {d: dev(pos["x"][d], y, z, c) for d in far_first},
           "y": {d: dev(x, pos["y"][d], z, c) for d in far_first},
           "z": {d: dev(x, y, pos["z"][d], c) for d in far_first}}
    here = {"x": x, "y": y, "z": z}
    sib = dev(x, y, z, 1 - c)

    def copy(src, dst, ssem, rsem, target):
        return pltpu.make_async_remote_copy(
            src_ref=src, dst_ref=dst, send_sem=ssem, recv_sem=rsem,
            device_id=target, device_id_type=MESH)

    def got(ref, sem):
        copy(ref, ref, sem, sem, sib).wait_recv()

    def left(ref, sem):
        copy(ref, ref, sem, sem, sib).wait_send()

    part = half // H
    fetch = []
    for h in range(H):
        src = dens.at[:, pl.ds(h * part, part)]
        fetch.append(pltpu.make_async_copy(src, a2.at[0, h, pl.ds(xs, slab)], in_s.at[2 * h]))
        fetch.append(pltpu.make_async_copy(
            src, a3.at[0, h, pl.ds(pl.multiple_of(y * slab, slab), slab)], in_s.at[2 * h + 1]))
    fetch.append(pltpu.make_async_copy(keep_in, keep, in_s.at[2 * H]))
    fetch.append(pltpu.make_async_copy(branches_in, branches, in_s.at[2 * H + 1]))
    for cp in fetch:
        cp.start()
    barrier = pltpu.get_barrier_semaphore()
    for d in far_first:
        for axis in ("x", "y", "z"):
            pl.semaphore_signal(barrier, inc=1, device_id=ids[axis][d], device_id_type=MESH)
    pl.semaphore_signal(barrier, inc=1, device_id=sib, device_id_type=MESH)
    for cp in fetch[:2 * H]:
        cp.wait()
    pl.semaphore_wait(barrier, 3 * (G - 1) + 1)

    line = a2.at[0, :, pl.ds(0, (G - 1) * slab)]

    def gather(p, axis, h):
        two = a2.at[p, h, pl.ds(xs, slab)]
        three = a3.at[p, h, pl.ds(pl.multiple_of(here[axis] * slab, slab), slab)]
        for d in far_first:
            copy(three, three, au_s, au_r.at[p], ids[axis][d]).start()
        for d in far_first:
            copy(two, two, ax_s, ax_r.at[p], ids["x"][d]).start()

    iota = functools.partial(lax.broadcasted_iota, jnp.int32)
    pick = jnp.where(iota((slab, half), 1) == x * slab - c * half + iota((slab, half), 0), 0.5, 0.0).astype(BF16)
    row_here = (x * slab) // half == c
    on_block = jnp.where(y == z, 1.0, 0.0).astype(F32)
    own_diag = jnp.where(iota((slab, half), 0) + x * slab == iota((slab, half), 1) + c * half, on_block, 0.0)

    t_one, t_two = [], []

    def across(ref, p, start, size):
        return jnp.concatenate([ref[p, k, pl.ds(start, size), :] for k in range(H)], axis=1)

    def note_traces(p):
        shard = across(a2, p, xs, slab).astype(F32)
        squares = jnp.sum(shard * shard, axis=0, keepdims=True)
        diagonal = jnp.sum(shard * own_diag, axis=0, keepdims=True)
        t_one.append(jnp.sum(diagonal, axis=1, keepdims=True))
        t_two.append(jnp.sum(squares, axis=1, keepdims=True))
        return squares, diagonal

    for h in range(H):
        gather(0, "y", h)
    note_traces(0)
    fetch[2 * H].wait()
    fetch[2 * H + 1].wait()

    for s in range(STEPS):
        p = s % 2
        n = 1 - p
        last = s == STEPS - 1
        au, av = ("y", "z") if p == 0 else ("z", "y")
        u, v = here[au], here[av]
        us = pl.multiple_of(u * slab, slab)
        vs_at = pl.multiple_of(v * slab, slab)

        if last:
            got(vx.at[pl.ds(0, G - 1)], vs_r.at[1])
            vz[z] = jnp.sum(vx[...], axis=0)
            for d in far_first:
                copy(vz.at[z], vz.at[z], vs_s.at[0], vs_r.at[0], ids["z"][d]).start()
        got(line, ax_r.at[p])
        got(line, au_r.at[p])
        rows3 = across(a3, p, 0, bs)
        for h in range(H):
            h1[p, h] = lax.dot_general(rows3, across(a2, p, pl.multiple_of(theirs + h * part, part), part), NT,
                                       preferred_element_type=F32).astype(BF16)
            copy(h1.at[p, h], d1.at[p, h], dd_s.at[p], dd_r.at[p, h], sib).start()
        if s > 0:
            left(line, rs_s)
        for h in range(H):
            n1[h] = lax.dot_general(rows3, across(a2, p, pl.multiple_of(mine + h * part, part), part), NT,
                                    preferred_element_type=F32) - (0.5 * on_block) * a3[p, h].astype(F32)
            got(d1.at[p, h], dd_r.at[p, h])
            p1[p, h] = (n1[h] + d1[p, h].astype(F32)).astype(BF16)
            for d in far_first:
                copy(p1.at[p, h, pl.ds(pl.multiple_of(pos[av][d] * slab, slab), slab)],
                     rr.at[p, h, v], rs_s, rs_r.at[p, h], ids[av][d]).start()

        @pl.when(row_here)
        def _():
            own3 = across(a3, p, vs_at, slab)
            for h in range(H):
                far = across(a2, p, pl.multiple_of(theirs + h * part, part), part)
                e = lax.dot_general(pick, far, NT, preferred_element_type=F32)
                own = lax.dot_general(own3, far, NT, preferred_element_type=F32)
                es[p, 0, h] = (2.0 * e).astype(BF16)
                es[p, 1, h] = (own - e).astype(BF16)
            copy(es.at[p], ed.at[p], es_s.at[p], es_r.at[p], sib).start()
            for h in range(H):
                near = across(a2, p, pl.multiple_of(mine + h * part, part), part)
                e = lax.dot_general(pick, near, NT, preferred_element_type=F32)
                cur[h] = 2.0 * e
                rr[p, h, v] = (n1[h, pl.ds(vs_at, slab), :] + d1[p, h, pl.ds(vs_at, slab), :].astype(F32)
                               - e).astype(BF16)

        left(line, ax_s)
        left(line, au_s)
        left(h1.at[p], dd_s.at[p])

        @pl.when(row_here)
        def _():
            left(es.at[p], es_s.at[p])

        @pl.when(jnp.logical_not(row_here))
        def _():
            got(ed.at[p], es_r.at[p])
            for h in range(H):
                cur[h] = ed[p, 0, h].astype(F32)
                rr[p, h, v] = (n1[h, pl.ds(vs_at, slab), :] + ed[p, 1, h].astype(F32)).astype(BF16)

        if last:
            got(vz.at[pl.ds(0, G - 1)], vs_r.at[0])
            vs[c] = jnp.sum(vz[...], axis=0)
            copy(vs.at[c], vs.at[c], sb_s, sb_r, sib).start()
            got(vs.at[0], sb_r)
            vy[y] = (vs[0] + vs[1])[:, :LANES]
            for d in far_first:
                copy(vy.at[y], vy.at[y], vs_s.at[2], vs_r.at[2], ids["y"][d]).start()
            mid = jnp.where(x * slab < half, vs[0], vs[1])
            f = branches[s].astype(F32)
            grown = f * mid[0:1, :] + (1.0 - f) * (2.0 * mid[1:2, :] - mid[0:1, :])
            shown = iota((slab, half), 1) == lax.rem(x * slab, half) + iota((slab, half), 0)
            column = jnp.sum(jnp.where(shown, grown, 0.0), axis=1, keepdims=True)
            eye = iota((slab, slab), 0) == iota((slab, slab), 1)
            occ[...] = jnp.sum(jnp.where(eye, column, 0.0), axis=0, keepdims=True)

        f = branches[s].astype(F32)
        fa, fb = 2.0 * f - 1.0, 2.0 - 2.0 * f
        tall = min(slab, B)
        cb = (u * bs + c * half) // B
        for h in range(H):
            at2, at3 = xs, pl.multiple_of(v * slab, slab)
            got(rr.at[p, h, pl.ds(0, G - 1)], rs_r.at[p, h])
            now = cur[h]
            grown = fa * (jnp.sum(rr[p, h].astype(F32), axis=0) + now) + fb * now
            if last:
                grown = jnp.where(v * bs + x * slab + iota((slab, part), 0)
                                  == u * bs + c * half + h * part + iota((slab, part), 1), 0.0, grown)
            for r in range(0, slab, tall):
                rb = (v * bs + x * slab + r) // B
                for q in range(part // B):
                    cs = slice(q * B, (q + 1) * B)
                    new = (grown[r:r + tall, cs] * keep[s, rb, cb + h * (part // B) + q].astype(F32)).astype(BF16)
                    if last:
                        out[r:r + tall, h * part + q * B:h * part + (q + 1) * B] = new
                    else:
                        a2[n, h, pl.ds(pl.multiple_of(at2 + r, tall), tall), cs] = new
                        a3[n, h, pl.ds(pl.multiple_of(at3 + r, tall), tall), cs] = new
            if s == STEPS - 2 and h == H - 1:
                squares, diagonal = note_traces(n)
                lane, deep = iota((1, half), 1), iota((8, half), 0)
                trow = jnp.zeros((1, half), F32)
                for i in range(STEPS):
                    trow = trow + jnp.where(lane == 2 * i, t_one[i], 0.0) + jnp.where(lane == 2 * i + 1, t_two[i], 0.0)
                vx[x] = (jnp.where(deep == 0, squares, 0.0) + jnp.where(deep == 1, diagonal, 0.0)
                         + jnp.where(deep == 2, trow, 0.0))
                for d in far_first:
                    copy(vx.at[x], vx.at[x], vs_s.at[1], vs_r.at[1], ids["x"][d]).start()
            if not last:
                gather(n, av, h)
        if s < STEPS - 2:
            note_traces(n)

    got(vy.at[pl.ds(0, G - 1)], vs_r.at[2])
    tr = jnp.sum(vy[...], axis=0)[2:3, :] * (1.0 / order)
    lane, deep = iota((STEPS, LANES), 1), iota((STEPS, LANES), 0)
    for k in range(2):
        traces[:, k:k + 1] = jnp.sum(jnp.where(lane == 2 * deep + k, tr, 0.0), axis=1, keepdims=True)
    left(line, rs_s)
    left(vx.at[pl.ds(0, G - 1)], vs_s.at[1])
    left(vz.at[pl.ds(0, G - 1)], vs_s.at[0])
    left(vy.at[pl.ds(0, G - 1)], vs_s.at[2])
    left(vs.at[0], sb_s)


def body(G, density, branches, keep):
    slab, half = density.shape
    bs, part = 2 * half, half // H
    v, dma = pltpu.VMEM, pltpu.SemaphoreType.DMA
    vmem, hbm = pl.BlockSpec(memory_space=pltpu.VMEM), pl.BlockSpec(memory_space=pltpu.HBM)
    purified, traces, occ = pl.pallas_call(
        functools.partial(kernel, G, bs),
        out_shape=(jax.ShapeDtypeStruct((slab, half), BF16),
                   jax.ShapeDtypeStruct((STEPS, 2), F32),
                   jax.ShapeDtypeStruct((1, slab), F32)),
        in_specs=[hbm, hbm, hbm],
        out_specs=(vmem, vmem, vmem),
        scratch_shapes=[
            v((2, H, bs, part), BF16), v((2, H, bs, part), BF16), v((2, H, bs, part), BF16), v((H, bs, part), F32),
            v((2, H, bs, part), BF16), v((2, H, bs, part), BF16), v((H, slab, part), F32),
            v((2, 2, H, slab, part), BF16), v((2, 2, H, slab, part), BF16),
            v((2, H, G, slab, part), BF16),
            v((G, 8, half), F32), v((G, 8, half), F32), v((2, 8, half), F32), v((G, 8, LANES), F32),
            pltpu.SMEM(branches.shape, jnp.int32), pltpu.SMEM(keep.shape, jnp.int32),
            dma((2 * H + 2,)), dma, dma((2,)), dma, dma((2,)), dma, dma((2, H)), dma((2,)), dma((2, H)),
            dma((2,)), dma((2,)), dma((3,)), dma((3,)), dma, dma,
        ],
        compiler_params=pltpu.CompilerParams(
            collective_id=0, has_side_effects=True, vmem_limit_bytes=55168 * 1024),
        name="purify",
    )(density, branches, keep)
    return purified, traces, occ.reshape(slab)


def solution(mesh):
    G = mesh.shape["col"] // 2
    return jax.shard_map(
        functools.partial(body, G),
        mesh=mesh,
        in_specs=(P("row", "col"), P(), P()),
        out_specs=(P("row", "col"), P(), P("row")),
        check_vma=False,
    )
```

```python
import functools

import jax
import jax.numpy as jnp
from jax import lax
from jax.experimental import pallas as pl
from jax.experimental.pallas import tpu as pltpu
from jax.sharding import PartitionSpec as P

B = 128
LANES = 128
STEPS = 4
H = 2
MESH = pl.DeviceIdType.MESH
F32 = jnp.float32
BF16 = jnp.bfloat16
NT = (((1,), (1,)), ((), ()))


def kernel(G, bs, dens, branches_in, keep_in, out, traces, occ,
           a2, a3, p1, n1, h1, d1, cur, es, ed, rr, vx, vz, vs, vy, branches, keep,
           in_s, ax_s, ax_r, au_s, au_r, rs_s, rs_r, dd_s, dd_r, es_s, es_r, vs_s, vs_r, sb_s, sb_r):
    half, slab = bs // 2, bs // G
    order = G * bs
    row, col = lax.axis_index("row"), lax.axis_index("col")
    x, y, z, c = lax.rem(row, G), row // G, col // 2, lax.rem(col, 2)
    xs = pl.multiple_of(x * slab, slab)
    mine = pl.multiple_of(c * half, half)
    theirs = pl.multiple_of((1 - c) * half, half)

    def dev(ax, ay, az, ac):
        return {"row": ay * G + ax, "col": az * 2 + ac}

    far_first = sorted(range(1, G), key=lambda d: -min(d, G - d))
    way = {d: d + c * (G - 2 * d) for d in far_first}
    pos = {"x": {d: lax.rem(x + way[d], G) for d in far_first},
           "y": {d: lax.rem(y + way[d], G) for d in far_first},
           "z": {d: lax.rem(z + way[d], G) for d in far_first}}
    ids = {"x": {d: dev(pos["x"][d], y, z, c) for d in far_first},
           "y": {d: dev(x, pos["y"][d], z, c) for d in far_first},
           "z": {d: dev(x, y, pos["z"][d], c) for d in far_first}}
    here = {"x": x, "y": y, "z": z}
    sib = dev(x, y, z, 1 - c)

    def copy(src, dst, ssem, rsem, target):
        return pltpu.make_async_remote_copy(
            src_ref=src, dst_ref=dst, send_sem=ssem, recv_sem=rsem,
            device_id=target, device_id_type=MESH)

    def got(ref, sem):
        copy(ref, ref, sem, sem, sib).wait_recv()

    def left(ref, sem):
        copy(ref, ref, sem, sem, sib).wait_send()

    part = half // H
    fetch = []
    for h in range(H):
        src = dens.at[:, pl.ds(h * part, part)]
        fetch.append(pltpu.make_async_copy(src, a2.at[0, h, pl.ds(xs, slab)], in_s.at[2 * h]))
        fetch.append(pltpu.make_async_copy(
            src, a3.at[0, h, pl.ds(pl.multiple_of(y * slab, slab), slab)], in_s.at[2 * h + 1]))
    fetch.append(pltpu.make_async_copy(keep_in, keep, in_s.at[2 * H]))
    fetch.append(pltpu.make_async_copy(branches_in, branches, in_s.at[2 * H + 1]))
    for cp in fetch:
        cp.start()
    barrier = pltpu.get_barrier_semaphore()
    for d in far_first:
        for axis in ("x", "y", "z"):
            pl.semaphore_signal(barrier, inc=1, device_id=ids[axis][d], device_id_type=MESH)
    pl.semaphore_signal(barrier, inc=1, device_id=sib, device_id_type=MESH)
    for cp in fetch[:2 * H]:
        cp.wait()
    pl.semaphore_wait(barrier, 3 * (G - 1) + 1)

    line = a2.at[0, :, pl.ds(0, (G - 1) * slab)]

    def gather(p, axis, h):
        two = a2.at[p, h, pl.ds(xs, slab)]
        three = a3.at[p, h, pl.ds(pl.multiple_of(here[axis] * slab, slab), slab)]
        for d in far_first:
            copy(three, three, au_s, au_r.at[p], ids[axis][d]).start()
        for d in far_first:
            copy(two, two, ax_s, ax_r.at[p], ids["x"][d]).start()

    iota = functools.partial(lax.broadcasted_iota, jnp.int32)
    pick = jnp.where(iota((slab, half), 1) == x * slab - c * half + iota((slab, half), 0), 0.5, 0.0).astype(BF16)
    row_here = (x * slab) // half == c
    on_block = jnp.where(y == z, 1.0, 0.0).astype(F32)
    own_diag = jnp.where(iota((slab, half), 0) + x * slab == iota((slab, half), 1) + c * half, on_block, 0.0)

    t_one, t_two = [], []

    def across(ref, p, start, size):
        return jnp.concatenate([ref[p, k, pl.ds(start, size), :] for k in range(H)], axis=1)

    def note_traces(p):
        shard = across(a2, p, xs, slab).astype(F32)
        squares = jnp.sum(shard * shard, axis=0, keepdims=True)
        diagonal = jnp.sum(shard * own_diag, axis=0, keepdims=True)
        t_one.append(jnp.sum(diagonal, axis=1, keepdims=True))
        t_two.append(jnp.sum(squares, axis=1, keepdims=True))
        return squares, diagonal

    for h in range(H):
        gather(0, "y", h)
    note_traces(0)
    fetch[2 * H].wait()
    fetch[2 * H + 1].wait()

    for s in range(STEPS):
        p = s % 2
        n = 1 - p
        last = s == STEPS - 1
        au, av = ("y", "z") if p == 0 else ("z", "y")
        u, v = here[au], here[av]
        us = pl.multiple_of(u * slab, slab)
        vs_at = pl.multiple_of(v * slab, slab)

        if last:
            got(vx.at[pl.ds(0, G - 1)], vs_r.at[1])
            vz[z] = jnp.sum(vx[...], axis=0)
            for d in far_first:
                copy(vz.at[z], vz.at[z], vs_s.at[0], vs_r.at[0], ids["z"][d]).start()
        got(line, ax_r.at[p])
        got(line, au_r.at[p])
        rows3 = across(a3, p, 0, bs)
        for h in range(H):
            h1[p, h] = lax.dot_general(rows3, across(a2, p, pl.multiple_of(theirs + h * part, part), part), NT,
                                       preferred_element_type=F32).astype(BF16)
            copy(h1.at[p, h], d1.at[p, h], dd_s.at[p], dd_r.at[p, h], sib).start()
        if s > 0:
            left(line, rs_s)
        for h in range(H):
            n1[h] = lax.dot_general(rows3, across(a2, p, pl.multiple_of(mine + h * part, part), part), NT,
                                    preferred_element_type=F32) - (0.5 * on_block) * a3[p, h].astype(F32)
            got(d1.at[p, h], dd_r.at[p, h])
            p1[p, h] = (n1[h] + d1[p, h].astype(F32)).astype(BF16)
            for d in far_first:
                copy(p1.at[p, h, pl.ds(pl.multiple_of(pos[av][d] * slab, slab), slab)],
                     rr.at[p, h, v], rs_s, rs_r.at[p, h], ids[av][d]).start()

        @pl.when(row_here)
        def _():
            own3 = across(a3, p, vs_at, slab)
            for h in range(H):
                far = across(a2, p, pl.multiple_of(theirs + h * part, part), part)
                e = lax.dot_general(pick, far, NT, preferred_element_type=F32)
                own = lax.dot_general(own3, far, NT, preferred_element_type=F32)
                es[p, 0, h] = (2.0 * e).astype(BF16)
                es[p, 1, h] = (own - e).astype(BF16)
            copy(es.at[p], ed.at[p], es_s.at[p], es_r.at[p], sib).start()
            for h in range(H):
                near = across(a2, p, pl.multiple_of(mine + h * part, part), part)
                e = lax.dot_general(pick, near, NT, preferred_element_type=F32)
                cur[h] = 2.0 * e
                rr[p, h, v] = (n1[h, pl.ds(vs_at, slab), :] + d1[p, h, pl.ds(vs_at, slab), :].astype(F32)
                               - e).astype(BF16)

        left(line, ax_s)
        left(line, au_s)
        left(h1.at[p], dd_s.at[p])

        @pl.when(row_here)
        def _():
            left(es.at[p], es_s.at[p])

        @pl.when(jnp.logical_not(row_here))
        def _():
            got(ed.at[p], es_r.at[p])
            for h in range(H):
                cur[h] = ed[p, 0, h].astype(F32)
                rr[p, h, v] = (n1[h, pl.ds(vs_at, slab), :] + ed[p, 1, h].astype(F32)).astype(BF16)

        if last:
            got(vz.at[pl.ds(0, G - 1)], vs_r.at[0])
            vs[c] = jnp.sum(vz[...], axis=0)
            copy(vs.at[c], vs.at[c], sb_s, sb_r, sib).start()
            got(vs.at[0], sb_r)
            vy[y] = (vs[0] + vs[1])[:, :LANES]
            for d in far_first:
                copy(vy.at[y], vy.at[y], vs_s.at[2], vs_r.at[2], ids["y"][d]).start()
            mid = jnp.where(x * slab < half, vs[0], vs[1])
            f = branches[s].astype(F32)
            grown = f * mid[0:1, :] + (1.0 - f) * (2.0 * mid[1:2, :] - mid[0:1, :])
            shown = iota((slab, half), 1) == lax.rem(x * slab, half) + iota((slab, half), 0)
            column = jnp.sum(jnp.where(shown, grown, 0.0), axis=1, keepdims=True)
            eye = iota((slab, slab), 0) == iota((slab, slab), 1)
            occ[...] = jnp.sum(jnp.where(eye, column, 0.0), axis=0, keepdims=True)

        f = branches[s].astype(F32)
        fa, fb = 2.0 * f - 1.0, 2.0 - 2.0 * f
        tall = min(slab, B)
        cb = (u * bs + c * half) // B
        for h in range(H):
            at2, at3 = xs, pl.multiple_of(v * slab, slab)
            got(rr.at[p, h, pl.ds(0, G - 1)], rs_r.at[p, h])
            now = cur[h]
            grown = fa * (jnp.sum(rr[p, h].astype(F32), axis=0) + now) + fb * now
            if last:
                grown = jnp.where(v * bs + x * slab + iota((slab, part), 0)
                                  == u * bs + c * half + h * part + iota((slab, part), 1), 0.0, grown)
            for r in range(0, slab, tall):
                rb = (v * bs + x * slab + r) // B
                for q in range(part // B):
                    cs = slice(q * B, (q + 1) * B)
                    new = (grown[r:r + tall, cs] * keep[s, rb, cb + h * (part // B) + q].astype(F32)).astype(BF16)
                    if last:
                        out[r:r + tall, h * part + q * B:h * part + (q + 1) * B] = new
                    else:
                        a2[n, h, pl.ds(pl.multiple_of(at2 + r, tall), tall), cs] = new
                        a3[n, h, pl.ds(pl.multiple_of(at3 + r, tall), tall), cs] = new
            if s == STEPS - 2 and h == H - 1:
                squares, diagonal = note_traces(n)
                lane, deep = iota((1, half), 1), iota((8, half), 0)
                trow = jnp.zeros((1, half), F32)
                for i in range(STEPS):
                    trow = trow + jnp.where(lane == 2 * i, t_one[i], 0.0) + jnp.where(lane == 2 * i + 1, t_two[i], 0.0)
                vx[x] = (jnp.where(deep == 0, squares, 0.0) + jnp.where(deep == 1, diagonal, 0.0)
                         + jnp.where(deep == 2, trow, 0.0))
                for d in far_first:
                    copy(vx.at[x], vx.at[x], vs_s.at[1], vs_r.at[1], ids["x"][d]).start()
            if not last:
                gather(n, av, h)
        if s < STEPS - 2:
            note_traces(n)

    got(vy.at[pl.ds(0, G - 1)], vs_r.at[2])
    tr = jnp.sum(vy[...], axis=0)[2:3, :] * (1.0 / order)
    lane, deep = iota((STEPS, LANES), 1), iota((STEPS, LANES), 0)
    for k in range(2):
        traces[:, k:k + 1] = jnp.sum(jnp.where(lane == 2 * deep + k, tr, 0.0), axis=1, keepdims=True)
    left(line, rs_s)
    left(vx.at[pl.ds(0, G - 1)], vs_s.at[1])
    left(vz.at[pl.ds(0, G - 1)], vs_s.at[0])
    left(vy.at[pl.ds(0, G - 1)], vs_s.at[2])
    left(vs.at[0], sb_s)


def body(G, density, branches, keep):
    slab, half = density.shape
    bs, part = 2 * half, half // H
    v, dma = pltpu.VMEM, pltpu.SemaphoreType.DMA
    vmem, hbm = pl.BlockSpec(memory_space=pltpu.VMEM), pl.BlockSpec(memory_space=pltpu.HBM)
    purified, traces, occ = pl.pallas_call(
        functools.partial(kernel, G, bs),
        out_shape=(jax.ShapeDtypeStruct((slab, half), BF16),
                   jax.ShapeDtypeStruct((STEPS, 2), F32),
                   jax.ShapeDtypeStruct((1, slab), F32)),
        in_specs=[hbm, hbm, hbm],
        out_specs=(vmem, vmem, vmem),
        scratch_shapes=[
            v((2, H, bs, part), BF16), v((2, H, bs, part), BF16), v((2, H, bs, part), BF16), v((H, bs, part), F32),
            v((2, H, bs, part), BF16), v((2, H, bs, part), BF16), v((H, slab, part), F32),
            v((2, 2, H, slab, part), BF16), v((2, 2, H, slab, part), BF16),
            v((2, H, G, slab, part), BF16),
            v((G, 8, half), F32), v((G, 8, half), F32), v((2, 8, half), F32), v((G, 8, LANES), F32),
            pltpu.SMEM(branches.shape, jnp.int32), pltpu.SMEM(keep.shape, jnp.int32),
            dma((2 * H + 2,)), dma, dma((2,)), dma, dma((2,)), dma, dma((2, H)), dma((2,)), dma((2, H)),
            dma((2,)), dma((2,)), dma((3,)), dma((3,)), dma, dma,
        ],
        compiler_params=pltpu.CompilerParams(
            collective_id=0, has_side_effects=True, vmem_limit_bytes=55168 * 1024),
        name="purify",
    )(density, branches, keep)
    return purified, traces, occ.reshape(slab)


def solution(mesh):
    G = mesh.shape["col"] // 2
    return jax.shard_map(
        functools.partial(body, G),
        mesh=mesh,
        in_specs=(P("row", "col"), P(), P()),
        out_specs=(P("row", "col"), P(), P("row")),
        check_vma=False,
    )
```
